32 devices in a mesh: group: 2 (over x), replica: 4 (over y, core), tensor: 4 (over z).
Axes of the slice: x: 2, y: 2, z: 4, core: 2. Of those that a mesh axis runs over, the one named last changes fastest.
Arguments:
- hidden_state_rows: bfloat16 [64, 8192], P(('group', 'replica'), 'tensor'), parts along dimension 0, may hold values from -6 to 6
- queries: bfloat16 [64, 64, 128], P(('group', 'replica'), 'tensor'), parts along dimension 0, may hold values from -150 to 150
- rotated_key_cache: bfloat16 [64, 8, 1024, 128], P(('group', 'replica'), 'tensor'), parts along dimension 0, may hold values from -6 to 6
- cached_value_rows: bfloat16 [64, 8, 1024, 128], P(('group', 'replica'), 'tensor'), parts along dimension 0, may hold values from -6 to 6
- lengths: int32 [64], P(('group', 'replica')), parts along dimension 0, may hold values from 2 to 1024, as said below
- row_adapter_index: int32 [64], P(('group', 'replica')), parts along dimension 0, may hold values from 0 to 63
- key_value_weight: bfloat16 [8192, 2, 1024], P(None, None, 'tensor'), may hold values from -0.0625 to 0.0625
- adapter_down_weight: bfloat16 [128, 8192, 32], P(('group', 'replica'), 'tensor'), parts along dimension 0, may hold values from -0.0625 to 0.0625
- adapter_up_weight: bfloat16 [128, 2, 16, 1024], P(('group', 'replica'), None, None, 'tensor'), parts along dimension 0, may hold values from -1.5 to 1.5
Outputs:
- attention: bfloat16 [64, 8192], P(('group', 'replica'), 'tensor'), parts along dimension 0
The draws below stay inside these ranges and needn't reach their ends.
There are 2 independent parts, one for each index of `group`. The reference program is written for one: setup_inputs(seed, part) draws one part's arguments, and reference() takes and returns one part's arrays. A program takes and returns all parts, laid end to end along the dimension named above; an argument that names none is the same for every part. Nothing has to cross between parts.
Inputs may be any that keep to these rules, and one draw needn't show every extreme that they name: `lengths`: the first of each 8 consecutive rows has all 1024 positions in use.
All inputs are finite; a program needn't handle non-finite values.
Results may differ from the reference program's by a relative error of at most 0.009.
Values may be sent and summed in bfloat16 or wider, within the bound.
A program may use at most 128 MiB of HBM per device.

```python
import math
import jax
import jax.numpy as jnp
import numpy as np
from jax import lax

MODEL_WIDTH = 8192
QH = 64
KEY_VALUE_HEADS = 8
HEAD_WIDTH = 128
ADAPTER_RANK = 16
ROWS_DEV = 8
CACHE = 1024
GROUP_ROWS = 32
GROUP_ADAPTERS = 64


def shared_keys(key):
    return jnp.clip(jax.random.normal(key, (GROUP_ROWS, KEY_VALUE_HEADS, CACHE, HEAD_WIDTH), jnp.float32), -6.0, 6.0)


def draw_rotated_key_cache(key, part):
    drawn = shared_keys(key)
    return drawn.astype(jnp.bfloat16)


def draw_queries(key, part):
    key = jax.random.fold_in(key, 12)
    entries = jnp.clip(jax.random.normal(key, (GROUP_ROWS, QH, HEAD_WIDTH), jnp.float32), -6.0, 6.0)
    return entries.astype(jnp.bfloat16)


def draw_lengths(key, part):
    key = jax.random.fold_in(key, 13)
    drawn = jax.random.randint(key, (GROUP_ROWS,), 2, CACHE + 1, dtype=jnp.int32)
    leading = jnp.arange(GROUP_ROWS, dtype=jnp.int32) % ROWS_DEV == 0
    return jnp.where(leading, CACHE, drawn).astype(jnp.int32)


def place_ends(entries, stream_key, least, top_value):
    longest = entries.shape.index(max(entries.shape))
    spots = []
    for shift in (0, 1):
        where = [jax.random.randint(jax.random.fold_in(stream_key, axis), (), 0, length) for axis, length in enumerate(entries.shape)]
        where[longest] = (where[longest] + shift) % entries.shape[longest]
        spots.append(tuple(where))
    return entries.at[spots[0]].set(least).at[spots[1]].set(top_value)


def level_of(key, shape, split, low, largest):
    loudness, own = 1.0, jax.random.fold_in(key, 6)
    for axis_at, parts in split:
        steps = jnp.exp(jax.random.uniform(jax.random.fold_in(own, axis_at), (parts,), jnp.float32, low / len(split), largest / len(split)))
        loudness = loudness * jnp.repeat(steps, shape[axis_at] // parts).reshape([-1 if axis == axis_at else 1 for axis in range(len(shape))])
    return loudness


def cumulative_ranks(number_of, slope):
    weights = [(1 << 20) // math.isqrt(rank ** slope) + 1 for rank in range(1, number_of + 1)]
    deviation = 1 + sum(weights) // (1 << 30)
    return np.cumsum(np.array([max(1, weight // deviation) for weight in weights]))


def ranked_ids(rng, extent, count, lean):
    grid = cumulative_ranks(count, lean)
    pick = jax.random.randint(jax.random.fold_in(rng, 1), extent, 0, int(grid[count - 1]))
    grade = jnp.searchsorted(jnp.asarray(grid, jnp.int32), pick, side="right")
    return jax.random.permutation(jax.random.fold_in(rng, 2), count)[grade].astype(jnp.int32)


def gaussian(key, shape, spread, most, cuts=(), held_as=jnp.bfloat16):
    entries = spread * jax.random.normal(key, shape, jnp.float32)
    if cuts:
        entries = entries * level_of(key, shape, cuts, -0.22, 0.18)
    return jnp.clip(entries, -most, most).astype(held_as)


def setup_inputs(seed: int = 0, part: int = 0) -> dict:
    streams_of = jax.random.split(jax.random.key(seed), 10)
    part_splits = jax.random.split(jax.random.fold_in(streams_of[9], part), 10)
    hidden_state_rows = gaussian(part_splits[0], (GROUP_ROWS, MODEL_WIDTH), 1.0, 6.0, ((0, 4), (1, 4)))
    queries = draw_queries(jax.random.fold_in(jax.random.fold_in(streams_of[9], part), 71), part)
    rotated_key_cache = draw_rotated_key_cache(jax.random.fold_in(jax.random.fold_in(streams_of[9], part), 71), part)
    cached_value_rows = gaussian(part_splits[3], (GROUP_ROWS, KEY_VALUE_HEADS, CACHE, HEAD_WIDTH), 1.0, 6.0, ((0, 4), (1, 4)))
    lengths = draw_lengths(jax.random.fold_in(jax.random.fold_in(streams_of[9], part), 71), part)
    row_adapter_index = place_ends(ranked_ids(part_splits[5], (GROUP_ROWS,), GROUP_ADAPTERS, 2), jax.random.fold_in(part_splits[5], 3), 0, GROUP_ADAPTERS - 1).astype(jnp.int32)
    key_value_weight = gaussian(streams_of[6], (MODEL_WIDTH, 2, KEY_VALUE_HEADS * HEAD_WIDTH), MODEL_WIDTH ** -0.5, 0.0625, ((2, 4),))
    adapter_down_weight = gaussian(part_splits[7], (GROUP_ADAPTERS, MODEL_WIDTH, 2 * ADAPTER_RANK), MODEL_WIDTH ** -0.5, 0.0625, ((0, 4), (1, 4)))
    adapter_up_weight = gaussian(part_splits[8], (GROUP_ADAPTERS, 2, ADAPTER_RANK, KEY_VALUE_HEADS * HEAD_WIDTH), ADAPTER_RANK ** -0.5, 1.5, ((0, 4), (3, 4)))
    return dict(hidden_state_rows=hidden_state_rows, queries=queries, rotated_key_cache=rotated_key_cache, cached_value_rows=cached_value_rows, lengths=lengths, row_adapter_index=row_adapter_index, key_value_weight=key_value_weight, adapter_down_weight=adapter_down_weight, adapter_up_weight=adapter_up_weight)


adapter_scale = 2.0


def rotate_keys(vectors, positions):
    half_size = HEAD_WIDTH // 2
    frequency = jnp.exp(jnp.arange(half_size, dtype=jnp.float32) * (-2.0 * math.log(500000.0) / HEAD_WIDTH))
    angles = positions.astype(jnp.float32)[:, None] * frequency[None, :]
    cosine = jnp.cos(angles)[:, None, :]
    sine = jnp.sin(angles)[:, None, :]
    front_part = vectors[..., :half_size]
    back_part = vectors[..., half_size:]
    return jnp.concatenate([front_part * cosine - back_part * sine, back_part * cosine + front_part * sine], axis=-1)


def reference(hidden_state_rows, queries, rotated_key_cache, cached_value_rows, lengths, row_adapter_index, key_value_weight, adapter_down_weight, adapter_up_weight):
    base_projection = jnp.dot(hidden_state_rows, key_value_weight.reshape(MODEL_WIDTH, 2 * KEY_VALUE_HEADS * HEAD_WIDTH), preferred_element_type=jnp.float32)

    def row_wise_update(items):
        single_row_input, adapter_number = items
        reduced_rank_state = jnp.dot(single_row_input, adapter_down_weight[adapter_number], preferred_element_type=jnp.float32)
        up_weight_block = adapter_up_weight[adapter_number].astype(jnp.float32)
        return jnp.einsum('pj,pjk->pk', reduced_rank_state.reshape(2, ADAPTER_RANK), up_weight_block, precision=lax.Precision.HIGHEST)

    adapter_update = lax.map(row_wise_update, (hidden_state_rows, row_adapter_index)).reshape(GROUP_ROWS, 2 * KEY_VALUE_HEADS * HEAD_WIDTH)
    projected_rows = (base_projection + adapter_scale * adapter_update).reshape(GROUP_ROWS, 2, KEY_VALUE_HEADS, HEAD_WIDTH)
    new_key = rotate_keys(projected_rows[:, 0], lengths).astype(jnp.bfloat16)
    new_value = projected_rows[:, 1].astype(jnp.bfloat16)
    group_size = QH // KEY_VALUE_HEADS
    score_scale = HEAD_WIDTH ** -0.5

    def attend(items):
        query_row, keys_row, values_row, key_fresh, value_fresh, length_row = items
        grouped = query_row.reshape(KEY_VALUE_HEADS, group_size, HEAD_WIDTH).astype(jnp.float32)
        scores = jnp.einsum('kgd,ktd->kgt', grouped, keys_row.astype(jnp.float32)) * score_scale
        visible = jnp.arange(CACHE, dtype=jnp.int32) < length_row
        scores = jnp.where(visible[None, None, :], scores, -1e30)
        fresh_score = jnp.einsum('kgd,kd->kg', grouped, key_fresh.astype(jnp.float32)) * score_scale
        peak_score = jnp.maximum(jnp.max(scores, axis=-1), fresh_score)
        weights_raw = jnp.exp(scores - peak_score[..., None])
        fresh_raw = jnp.exp(fresh_score - peak_score)
        denominator = jnp.sum(weights_raw, axis=-1) + fresh_raw
        weights = (weights_raw / denominator[..., None]).astype(jnp.bfloat16)
        fresh_weight = (fresh_raw / denominator).astype(jnp.bfloat16)
        mixed = jnp.einsum('kgt,ktd->kgd', weights.astype(jnp.float32), values_row.astype(jnp.float32))
        mixed = mixed + fresh_weight.astype(jnp.float32)[..., None] * value_fresh.astype(jnp.float32)[:, None, :]
        return mixed.reshape(QH * HEAD_WIDTH).astype(jnp.bfloat16)

    return lax.map(attend, (queries, rotated_key_cache, cached_value_rows, new_key, new_value, lengths))
```

```python
import functools
import math

import jax
import jax.numpy as jnp
from jax import lax
from jax.experimental import pallas as pl
from jax.experimental.pallas import tpu as pltpu
from jax.sharding import PartitionSpec as P

adapter_scale = 2.0
LANES = 128


def rotate_keys(vectors, positions):
    head_width = vectors.shape[-1]
    half_size = head_width // 2
    frequency = jnp.exp(
        jnp.arange(half_size, dtype=jnp.float32) * (-2.0 * math.log(500000.0) / head_width)
    )
    angles = positions.astype(jnp.float32)[:, None] * frequency[None, :]
    cosine = jnp.cos(angles)[:, None, :]
    sine = jnp.sin(angles)[:, None, :]
    front_part = vectors[..., :half_size]
    back_part = vectors[..., half_size:]
    return jnp.concatenate(
        [front_part * cosine - back_part * sine, back_part * cosine + front_part * sine], axis=-1
    )


def dot(a, b):
    return jnp.dot(a, b, preferred_element_type=jnp.float32)


def project_kernel(
    tensor_size, replica_size, pieces,
    h_ref, ids_ref, weight_hbm, down_hbm, up_hbm, out_ref,
    hs_own, hs_t, hs_r, ids_r, weight, down, up, expanded, total,
    low_own, low_rx, delta_tx, delta_rx,
    load_sem, send_sem, recv_sem,
):
    rows, local = h_ref.shape
    blocks = local // LANES
    half_blocks = blocks // 2
    band = rows * pieces
    wide = LANES * pieces
    half_depth = half_blocks * wide
    shard_depth = 2 * half_depth
    rank2 = 32
    adapters = down.shape[0] // rank2
    per_tile = LANES // rank2
    tiles = adapters // per_tile

    me_t = lax.axis_index("tensor")
    me_r = lax.axis_index("replica")

    def t_at(step):
        return lax.rem(me_t + step + tensor_size, tensor_size)

    def r_at(step):
        return lax.rem(me_r + step + replica_size, replica_size)

    loads = [
        pltpu.make_async_copy(down_hbm, down, load_sem.at[0]),
        pltpu.make_async_copy(up_hbm, up, load_sem.at[1]),
    ]
    for d in range(tensor_size):
        source = pl.ds(pl.multiple_of(t_at(-d) * shard_depth, shard_depth), shard_depth)
        loads.append(
            pltpu.make_async_copy(weight_hbm.at[source], weight.at[d], load_sem.at[2 + d])
        )
    for load in loads:
        load.start()

    barrier = pltpu.get_barrier_semaphore()
    for d in range(1, tensor_size):
        pl.semaphore_signal(barrier, inc=1, device_id={"tensor": t_at(d)},
                            device_id_type=pl.DeviceIdType.MESH)
    for d in range(1, replica_size):
        pl.semaphore_signal(barrier, inc=1, device_id={"replica": r_at(d)},
                            device_id_type=pl.DeviceIdType.MESH)

    h32 = h_ref[...].astype(jnp.float32)
    hs_own[...] = jnp.concatenate(
        [h32[:, b * LANES:(b + 1) * LANES] for b in range(blocks)], axis=0
    ).astype(jnp.bfloat16)
    pl.semaphore_wait(barrier, tensor_size + replica_size - 2)

    count = [0]

    def remote(source, target, device):
        slot = count[0]
        count[0] += 1
        copy = pltpu.make_async_remote_copy(
            src_ref=source, dst_ref=target, send_sem=send_sem.at[slot],
            recv_sem=recv_sem.at[slot], device_id=device,
            device_id_type=pl.DeviceIdType.MESH,
        )
        copy.start()
        return copy

    ids_copies = [
        remote(ids_ref, ids_r.at[d - 1], {"replica": r_at(d)}) for d in range(1, replica_size)
    ]
    r_copies = [
        remote(hs_own, hs_r.at[d - 1], {"replica": r_at(d)}) for d in range(1, replica_size)
    ]
    t_copies = [
        remote(hs_own, hs_t.at[d - 1], {"tensor": t_at(d)}) for d in range(1, tensor_size)
    ]

    lane_of = lax.broadcasted_iota(jnp.int32, (rows, wide), 1)
    piece_shift = pieces.bit_length() - 1
    row_of = lax.broadcasted_iota(jnp.int32, (LANES, wide), 0)
    column_of = lax.broadcasted_iota(jnp.int32, (LANES, wide), 1)
    spread = jnp.where(
        lax.shift_right_logical(column_of, piece_shift) == row_of, 1.0, 0.0
    ).astype(jnp.bfloat16)
    piece_of = lane_of & (pieces - 1)

    def expand(source, d):
        repeated = dot(source, spread)
        for b in range(blocks):
            one = repeated[b * rows:(b + 1) * rows]
            parts = [jnp.where(piece_of == j, one, 0.0) for j in range(pieces)]
            half, at = divmod(b, half_blocks)
            expanded[d, half * band:(half + 1) * band, at * wide:(at + 1) * wide] = (
                jnp.concatenate(parts, axis=0).astype(jnp.bfloat16)
            )

    chunk = min(1024, half_depth)

    def accumulate(d):
        loads[2 + d].wait()

        def body(i, acc):
            at = pl.multiple_of(i * chunk, chunk)
            right = jnp.concatenate(
                [weight[d, pl.ds(at, chunk), :], weight[d, pl.ds(half_depth + at, chunk), :]],
                axis=1,
            )
            return acc + dot(expanded[d, :, pl.ds(at, chunk)], right)

        total[...] = lax.fori_loop(0, half_depth // chunk, body, total[...])

    total[...] = jnp.zeros_like(total)
    expand(hs_own[...], 0)

    loads[0].wait()
    for copy in ids_copies + r_copies:
        copy.wait_recv()
    stacks = [hs_own[...].astype(jnp.float32)] + [
        hs_r[d - 1].astype(jnp.float32) for d in range(1, replica_size)
    ]
    all_rows = jnp.concatenate(
        [
            jnp.concatenate([s[b * rows:(b + 1) * rows] for s in stacks], axis=0).astype(
                jnp.bfloat16
            )
            for b in range(blocks)
        ],
        axis=1,
    )
    low_all = lax.dot_general(
        all_rows, down[...], (((1,), (1,)), ((), ())), preferred_element_type=jnp.float32
    )
    ids = jnp.concatenate(
        [ids_ref[...]] + [ids_r[d - 1] for d in range(1, replica_size)], axis=0
    ) - me_r * adapters
    lane = lax.broadcasted_iota(jnp.int32, ids.shape, 1)
    adapter_of = lax.shift_right_logical(lane, rank2.bit_length() - 1)
    chosen = [ids == adapter_of + k * per_tile for k in range(tiles)]
    low = jnp.zeros(ids.shape, jnp.float32)
    for k in range(tiles):
        low = low + jnp.where(chosen[k], low_all[:, k * LANES:(k + 1) * LANES], 0.0)
    low_own[...] = low
    low_copies = [
        remote(low_own, low_rx.at[d - 1], {"tensor": t_at(d)}) for d in range(1, tensor_size)
    ]

    accumulate(0)

    loads[1].wait()
    for copy in low_copies:
        copy.wait_recv()
    for d in range(1, tensor_size):
        low = low + low_rx[d - 1]
    spread_low = jnp.concatenate([jnp.where(chosen[k], low, 0.0) for k in range(tiles)], axis=1)
    which = lax.broadcasted_iota(jnp.int32, spread_low.shape, 1) & (rank2 - 1)
    first = which < rank2 // 2
    left = jnp.concatenate(
        [jnp.where(first, spread_low, 0.0), jnp.where(first, 0.0, spread_low)], axis=0
    )
    top = left.astype(jnp.bfloat16)
    rest = left - top.astype(jnp.float32)
    middle = rest.astype(jnp.bfloat16)
    bottom = (rest - middle.astype(jnp.float32)).astype(jnp.bfloat16)
    delta = dot(top, up[...]) + (dot(middle, up[...]) + dot(bottom, up[...]))
    group_rows = rows * replica_size
    for d in range(replica_size):
        delta_tx[d] = jnp.concatenate(
            [
                delta[
                    (j % 2) * group_rows + d * rows:(j % 2) * group_rows + (d + 1) * rows,
                    (j // 2) * LANES:(j // 2 + 1) * LANES,
                ]
                for j in range(pieces)
            ],
            axis=0,
        )
    delta_copies = [
        remote(delta_tx.at[d], delta_rx.at[d - 1], {"replica": r_at(-d)})
        for d in range(1, replica_size)
    ]

    for d in range(1, tensor_size):
        t_copies[d - 1].wait_recv()
        expand(hs_t[d - 1], d)
        accumulate(d)

    result = total[0:band, 0:LANES] + total[band:2 * band, LANES:2 * LANES]
    update = delta_tx[0]
    for d in range(1, replica_size):
        delta_copies[d - 1].wait_recv()
        update = update + delta_rx[d - 1]
    out_ref[...] = result + adapter_scale * update
    for copy in ids_copies + r_copies + t_copies + low_copies + delta_copies:
        copy.wait_send()


def project(tensor_size, replica_size, hidden, ids, weight, down, up):
    rows, local = hidden.shape
    width = weight.shape[0]
    pieces = weight.shape[1] * weight.shape[2] // LANES
    blocks = local // LANES
    band = rows * pieces
    weight = (
        weight.reshape(width, 2, pieces // 2, LANES)
        .transpose(0, 2, 1, 3)
        .reshape(width * pieces, LANES)
    )
    adapters, _, rank2 = down.shape
    down = down.transpose(0, 2, 1).reshape(adapters * rank2, local)
    up = up.reshape(adapters * rank2, up.shape[3])
    ids = jnp.broadcast_to(ids[:, None], (rows, LANES))
    t1, r1 = tensor_size - 1, replica_size - 1
    copies = 2 * t1 + 3 * r1
    vmem = pl.BlockSpec(memory_space=pltpu.VMEM)
    hbm = pl.BlockSpec(memory_space=pl.ANY)
    stack = (blocks * rows, LANES)
    group_rows = rows * replica_size
    return pl.pallas_call(
        functools.partial(project_kernel, tensor_size, replica_size, pieces),
        out_shape=jax.ShapeDtypeStruct((band, LANES), jnp.float32),
        in_specs=[vmem, vmem, hbm, hbm, hbm],
        out_specs=vmem,
        scratch_shapes=[
            pltpu.VMEM(stack, jnp.bfloat16),
            pltpu.VMEM((t1,) + stack, jnp.bfloat16),
            pltpu.VMEM((r1,) + stack, jnp.bfloat16),
            pltpu.VMEM((r1, rows, LANES), jnp.int32),
            pltpu.VMEM((tensor_size, local * pieces, LANES), jnp.bfloat16),
            pltpu.VMEM(down.shape, jnp.bfloat16),
            pltpu.VMEM(up.shape, jnp.bfloat16),
            pltpu.VMEM((tensor_size, 2 * band, local * pieces // 2), jnp.bfloat16),
            pltpu.VMEM((2 * band, 2 * LANES), jnp.float32),
            pltpu.VMEM((group_rows, LANES), jnp.float32),
            pltpu.VMEM((t1, group_rows, LANES), jnp.float32),
            pltpu.VMEM((replica_size, band, LANES), jnp.float32),
            pltpu.VMEM((r1, band, LANES), jnp.float32),
            pltpu.SemaphoreType.DMA((2 + tensor_size,)),
            pltpu.SemaphoreType.DMA((copies,)),
            pltpu.SemaphoreType.DMA((copies,)),
        ],
        compiler_params=pltpu.CompilerParams(
            collective_id=0, has_side_effects=True, vmem_limit_bytes=30 << 20
        ),
        cost_estimate=pl.CostEstimate(
            flops=2 * rows * width * pieces * LANES,
            bytes_accessed=2 * (weight.size + down.size + up.size),
            transcendentals=0,
        ),
    )(hidden, ids, weight, down, up)


def on_device(
    tensor_size,
    replica_size,
    hidden_state_rows,
    queries,
    rotated_key_cache,
    cached_value_rows,
    lengths,
    row_adapter_index,
    key_value_weight,
    adapter_down_weight,
    adapter_up_weight,
):
    request_row_count = hidden_state_rows.shape[0]
    shard_heads = rotated_key_cache.shape[1]
    head_width = rotated_key_cache.shape[3]
    projected = project(
        tensor_size,
        replica_size,
        hidden_state_rows,
        row_adapter_index,
        key_value_weight,
        adapter_down_weight,
        adapter_up_weight,
    )
    projected_rows = projected.reshape(
        shard_heads, 2, request_row_count, head_width
    ).transpose(2, 1, 0, 3)
    new_key = rotate_keys(projected_rows[:, 0], lengths).astype(jnp.bfloat16)
    new_value = projected_rows[:, 1].astype(jnp.bfloat16)
    group_size = queries.shape[1] // shard_heads
    score_scale = head_width ** (-0.5)
    grouped = queries.reshape(request_row_count, shard_heads, group_size, head_width)
    cache_length = rotated_key_cache.shape[2]
    scores = (
        jnp.einsum(
            "rkgd,rktd->rkgt", grouped, rotated_key_cache, preferred_element_type=jnp.float32
        )
        * score_scale
    )
    visible = jnp.arange(cache_length, dtype=jnp.int32)[None, :] < lengths[:, None]
    scores = jnp.where(visible[:, None, None, :], scores, -1e30)
    fresh_score = (
        jnp.einsum("rkgd,rkd->rkg", grouped, new_key, preferred_element_type=jnp.float32)
        * score_scale
    )
    peak_score = jnp.maximum(jnp.max(scores, axis=-1), fresh_score)
    weights_raw = jnp.exp(scores - peak_score[..., None])
    fresh_raw = jnp.exp(fresh_score - peak_score)
    denominator = jnp.sum(weights_raw, axis=-1) + fresh_raw
    weights = (weights_raw / denominator[..., None]).astype(jnp.bfloat16)
    fresh_weight = (fresh_raw / denominator).astype(jnp.bfloat16)
    mixed = jnp.einsum(
        "rkgt,rktd->rkgd", weights, cached_value_rows, preferred_element_type=jnp.float32
    )
    mixed = (
        mixed
        + fresh_weight.astype(jnp.float32)[..., None] * new_value.astype(jnp.float32)[:, :, None, :]
    )
    return mixed.reshape(request_row_count, shard_heads * group_size * head_width).astype(
        jnp.bfloat16
    )


def solution(mesh):
    in_specs = (
        P(("group", "replica"), "tensor"),
        P(("group", "replica"), "tensor", None),
        P(("group", "replica"), "tensor", None, None),
        P(("group", "replica"), "tensor", None, None),
        P(("group", "replica")),
        P(("group", "replica")),
        P(None, None, "tensor"),
        P(("group", "replica"), "tensor", None),
        P(("group", "replica"), None, None, "tensor"),
    )
    out_specs = P(("group", "replica"), "tensor")
    body = functools.partial(on_device, mesh.shape["tensor"], mesh.shape["replica"])
    return jax.shard_map(
        body, mesh=mesh, in_specs=in_specs, out_specs=out_specs, check_vma=False
    )
```

```python
import functools
import math

import jax
import jax.numpy as jnp
from jax import lax
from jax.experimental import pallas as pl
from jax.experimental.pallas import tpu as pltpu
from jax.sharding import PartitionSpec as P

adapter_scale = 2.0
LANES = 128


def rotate_keys(vectors, cosine, sine):
    half_size = vectors.shape[1] // 2
    lane = lax.broadcasted_iota(jnp.int32, vectors.shape, 1)
    swapped = pltpu.roll(vectors, half_size, 1)
    return vectors * cosine + jnp.where(lane < half_size, -swapped, swapped) * sine


def dot(a, b):
    return jnp.dot(a, b, preferred_element_type=jnp.float32)


def project_kernel(
    tensor_size, replica_size, pieces,
    h_ref, query_ref, lengths_ref, index_ref, key_hbm, value_hbm, weight_hbm, down_hbm, up_hbm,
    out_ref, ids_ref, keys, values, query32, mixed, peak, mass, hs_own, hs_t, hs_r, ids_r, weight, down, up, expanded, total,
    low_own, low_rx, delta_tx, delta_rx,
    load_sem, send_sem, recv_sem,
):
    rows, local = h_ref.shape
    blocks = local // LANES
    half_blocks = blocks // 2
    band = rows * pieces
    wide = LANES * pieces
    half_depth = half_blocks * wide
    shard_depth = 2 * half_depth
    rank2 = 32
    adapters = down.shape[0] // rank2
    per_tile = LANES // rank2
    tiles = adapters // per_tile

    me_t = lax.axis_index("tensor")
    me_r = lax.axis_index("replica")

    def t_at(step):
        return lax.rem(me_t + step + tensor_size, tensor_size)

    def r_at(step):
        return lax.rem(me_r + step + replica_size, replica_size)

    loads = [
        pltpu.make_async_copy(down_hbm, down, load_sem.at[0]),
        pltpu.make_async_copy(up_hbm, up, load_sem.at[1]),
    ]
    for d in range(tensor_size):
        source = pl.ds(pl.multiple_of(t_at(-d) * shard_depth, shard_depth), shard_depth)
        loads.append(
            pltpu.make_async_copy(weight_hbm.at[source], weight.at[d], load_sem.at[2 + d])
        )
    heads = keys.shape[1]
    row_half = rows // 2
    cache_loads = []
    for part in range(2):
        span = pl.ds(part * row_half, row_half)
        for source, target in ((key_hbm, keys), (value_hbm, values)):
            cache_loads.append(
                pltpu.make_async_copy(
                    source.at[span], target.at[span],
                    load_sem.at[2 + tensor_size + len(cache_loads)],
                )
            )
    for load in loads[:2] + cache_loads + loads[2:]:
        load.start()

    barrier = pltpu.get_barrier_semaphore()
    for d in range(1, tensor_size):
        pl.semaphore_signal(barrier, inc=1, device_id={"tensor": t_at(d)},
                            device_id_type=pl.DeviceIdType.MESH)
    for d in range(1, replica_size):
        pl.semaphore_signal(barrier, inc=1, device_id={"replica": r_at(d)},
                            device_id_type=pl.DeviceIdType.MESH)

    h32 = h_ref[...].astype(jnp.float32)
    hs_own[...] = jnp.concatenate(
        [h32[:, b * LANES:(b + 1) * LANES] for b in range(blocks)], axis=0
    ).astype(jnp.bfloat16)
    for r in range(rows):
        ids_ref[r:r + 1, :] = jnp.full((1, LANES), index_ref[r], jnp.int32)
    pl.semaphore_wait(barrier, tensor_size + replica_size - 2)

    count = [0]

    def remote(source, target, device):
        slot = count[0]
        count[0] += 1
        copy = pltpu.make_async_remote_copy(
            src_ref=source, dst_ref=target, send_sem=send_sem.at[slot],
            recv_sem=recv_sem.at[slot], device_id=device,
            device_id_type=pl.DeviceIdType.MESH,
        )
        copy.start()
        return copy

    ids_copies = [
        remote(ids_ref, ids_r.at[d - 1], {"replica": r_at(d)}) for d in range(1, replica_size)
    ]
    r_copies = [
        remote(hs_own, hs_r.at[d - 1], {"replica": r_at(d)}) for d in range(1, replica_size)
    ]
    t_copies = [
        remote(hs_own, hs_t.at[d - 1], {"tensor": t_at(d)}) for d in range(1, tensor_size)
    ]

    lane_of = lax.broadcasted_iota(jnp.int32, (rows, wide), 1)
    piece_shift = pieces.bit_length() - 1
    row_of = lax.broadcasted_iota(jnp.int32, (LANES, wide), 0)
    column_of = lax.broadcasted_iota(jnp.int32, (LANES, wide), 1)
    spread = jnp.where(
        lax.shift_right_logical(column_of, piece_shift) == row_of, 1.0, 0.0
    ).astype(jnp.bfloat16)
    piece_of = lane_of & (pieces - 1)

    def expand(source, d):
        repeated = dot(source, spread)
        for b in range(blocks):
            one = repeated[b * rows:(b + 1) * rows]
            parts = [jnp.where(piece_of == j, one, 0.0) for j in range(pieces)]
            half, at = divmod(b, half_blocks)
            expanded[d, half * band:(half + 1) * band, at * wide:(at + 1) * wide] = (
                jnp.concatenate(parts, axis=0).astype(jnp.bfloat16)
            )

    chunk = min(1024, half_depth)

    def accumulate(d):
        loads[2 + d].wait()

        def body(i, acc):
            at = pl.multiple_of(i * chunk, chunk)
            right = jnp.concatenate(
                [weight[d, pl.ds(at, chunk), :], weight[d, pl.ds(half_depth + at, chunk), :]],
                axis=1,
            )
            return acc + dot(expanded[d, :, pl.ds(at, chunk)], right)

        total[...] = lax.fori_loop(0, half_depth // chunk, body, total[...])

    group_size = query_ref.shape[1] // heads
    head_width = query_ref.shape[2]
    cache = keys.shape[2]
    scale = head_width ** (-0.5)

    def attend(r):
        query = query_ref[r].astype(jnp.float32)
        query32[r] = query
        if heads > 1:
            owner = lax.broadcasted_iota(jnp.int32, query.shape, 0)
            query = jnp.concatenate(
                [
                    jnp.where(
                        (owner >= c * group_size) & (owner < (c + 1) * group_size), query, 0.0
                    )
                    for c in range(heads)
                ],
                axis=1,
            )
        key_row = jnp.concatenate([keys[r, c] for c in range(heads)], axis=1)
        value_row = jnp.concatenate([values[r, c] for c in range(heads)], axis=1)
        scores = lax.dot_general(
            query.astype(jnp.bfloat16), key_row, (((1,), (1,)), ((), ())),
            preferred_element_type=jnp.float32,
        ) * scale
        position = lax.broadcasted_iota(jnp.int32, scores.shape, 1)
        scores = jnp.where(position < lengths_ref[r], scores, -1e30)
        top = jnp.max(scores, axis=1, keepdims=True)
        raw = jnp.exp(scores - top)
        both = dot(raw.astype(jnp.bfloat16), value_row)
        mixed[r] = jnp.concatenate(
            [
                both[c * group_size:(c + 1) * group_size, c * head_width:(c + 1) * head_width]
                for c in range(heads)
            ],
            axis=0,
        )
        wide_shape = (heads * group_size, head_width)
        peak[r] = jnp.broadcast_to(top, wide_shape)
        mass[r] = jnp.broadcast_to(jnp.sum(raw, axis=1, keepdims=True), wide_shape)

    total[...] = jnp.zeros_like(total)
    expand(hs_own[...], 0)

    for load in cache_loads[:2]:
        load.wait()
    for r in range(row_half):
        attend(r)

    loads[0].wait()
    for copy in ids_copies + r_copies:
        copy.wait_recv()
    stacks = [hs_own[...].astype(jnp.float32)] + [
        hs_r[d - 1].astype(jnp.float32) for d in range(1, replica_size)
    ]
    all_rows = jnp.concatenate(
        [
            jnp.concatenate([s[b * rows:(b + 1) * rows] for s in stacks], axis=0).astype(
                jnp.bfloat16
            )
            for b in range(blocks)
        ],
        axis=1,
    )
    low_all = lax.dot_general(
        all_rows, down[...], (((1,), (1,)), ((), ())), preferred_element_type=jnp.float32
    )
    ids = jnp.concatenate(
        [ids_ref[...]] + [ids_r[d - 1] for d in range(1, replica_size)], axis=0
    ) - me_r * adapters
    lane = lax.broadcasted_iota(jnp.int32, ids.shape, 1)
    adapter_of = lax.shift_right_logical(lane, rank2.bit_length() - 1)
    chosen = [ids == adapter_of + k * per_tile for k in range(tiles)]
    low = jnp.zeros(ids.shape, jnp.float32)
    for k in range(tiles):
        low = low + jnp.where(chosen[k], low_all[:, k * LANES:(k + 1) * LANES], 0.0)
    low_own[...] = low
    low_copies = [
        remote(low_own, low_rx.at[d - 1], {"tensor": t_at(d)}) for d in range(1, tensor_size)
    ]

    for load in cache_loads[2:]:
        load.wait()
    for r in range(row_half, rows):
        attend(r)

    loads[1].wait()
    for copy in low_copies:
        copy.wait_recv()
    for d in range(1, tensor_size):
        low = low + low_rx[d - 1]
    spread_low = jnp.concatenate([jnp.where(chosen[k], low, 0.0) for k in range(tiles)], axis=1)
    which = lax.broadcasted_iota(jnp.int32, spread_low.shape, 1) & (rank2 - 1)
    first = which < rank2 // 2
    left = jnp.concatenate(
        [jnp.where(first, spread_low, 0.0), jnp.where(first, 0.0, spread_low)], axis=0
    )
    top = left.astype(jnp.bfloat16)
    rest = left - top.astype(jnp.float32)
    middle = rest.astype(jnp.bfloat16)
    bottom = (rest - middle.astype(jnp.float32)).astype(jnp.bfloat16)
    delta = dot(top, up[...]) + (dot(middle, up[...]) + dot(bottom, up[...]))
    group_rows = rows * replica_size
    for d in range(replica_size):
        delta_tx[d] = jnp.concatenate(
            [
                delta[
                    (j % 2) * group_rows + d * rows:(j % 2) * group_rows + (d + 1) * rows,
                    (j // 2) * LANES:(j // 2 + 1) * LANES,
                ]
                for j in range(pieces)
            ],
            axis=0,
        )
    delta_copies = [
        remote(delta_tx.at[d], delta_rx.at[d - 1], {"replica": r_at(-d)})
        for d in range(1, replica_size)
    ]

    accumulate(0)
    for d in range(1, tensor_size):
        t_copies[d - 1].wait_recv()
        expand(hs_t[d - 1], d)
        accumulate(d)

    result = total[0:band, 0:LANES] + total[band:2 * band, LANES:2 * LANES]
    update = delta_tx[0]
    for d in range(1, replica_size):
        delta_copies[d - 1].wait_recv()
        update = update + delta_rx[d - 1]
    projected = result + adapter_scale * update

    position = jnp.concatenate(
        [jnp.full((1, head_width), lengths_ref[r], jnp.int32) for r in range(rows)], axis=0
    ).astype(jnp.float32)
    lane = lax.broadcasted_iota(jnp.int32, (rows, head_width), 1) & (head_width // 2 - 1)
    frequency = jnp.exp(lane.astype(jnp.float32) * (-2.0 * math.log(500000.0) / head_width))
    cosine, sine = jnp.cos(position * frequency), jnp.sin(position * frequency)
    outputs = []
    for c in range(heads):
        at = 2 * c * rows
        new_key = rotate_keys(projected[at:at + rows], cosine, sine)
        new_key = new_key.astype(jnp.bfloat16).astype(jnp.float32)
        new_value = projected[at + rows:at + 2 * rows].astype(jnp.bfloat16).astype(jnp.float32)
        for h in range(c * group_size, (c + 1) * group_size):
            fresh = jnp.sum(query32[:, h, :] * new_key, axis=1, keepdims=True) * scale
            old_peak = peak[:, h, :]
            new_peak = jnp.maximum(old_peak, fresh)
            keep = jnp.exp(old_peak - new_peak)
            fresh_raw = jnp.exp(fresh - new_peak)
            outputs.append(
                (mixed[:, h, :] * keep + fresh_raw * new_value)
                / (mass[:, h, :] * keep + fresh_raw)
            )
    out_ref[...] = jnp.concatenate(outputs, axis=1).astype(out_ref.dtype)
    for copy in ids_copies + r_copies + t_copies + low_copies + delta_copies:
        copy.wait_send()


def project(tensor_size, replica_size, hidden, queries, keys, values, lengths, ids, weight, down, up):
    rows, local = hidden.shape
    width = weight.shape[0]
    pieces = weight.shape[1] * weight.shape[2] // LANES
    blocks = local // LANES
    band = rows * pieces
    weight = (
        weight.reshape(width, 2, pieces // 2, LANES)
        .transpose(0, 2, 1, 3)
        .reshape(width * pieces, LANES)
    )
    adapters, _, rank2 = down.shape
    down = down.transpose(0, 2, 1).reshape(adapters * rank2, local)
    up = up.reshape(adapters * rank2, up.shape[3])
    t1, r1 = tensor_size - 1, replica_size - 1
    copies = 2 * t1 + 3 * r1
    vmem = pl.BlockSpec(memory_space=pltpu.VMEM)
    smem = pl.BlockSpec(memory_space=pltpu.SMEM)
    hbm = pl.BlockSpec(memory_space=pl.ANY)
    stack = (blocks * rows, LANES)
    group_rows = rows * replica_size
    return pl.pallas_call(
        functools.partial(project_kernel, tensor_size, replica_size, pieces),
        out_shape=jax.ShapeDtypeStruct(
            (rows, queries.shape[1] * queries.shape[2]), jnp.bfloat16
        ),
        in_specs=[vmem, vmem, smem, smem, hbm, hbm, hbm, hbm, hbm],
        out_specs=vmem,
        scratch_shapes=[
            pltpu.VMEM((rows, LANES), jnp.int32),
            pltpu.VMEM(keys.shape, jnp.bfloat16),
            pltpu.VMEM(values.shape, jnp.bfloat16),
            pltpu.VMEM(queries.shape, jnp.float32),
            pltpu.VMEM(queries.shape, jnp.float32),
            pltpu.VMEM(queries.shape, jnp.float32),
            pltpu.VMEM(queries.shape, jnp.float32),
            pltpu.VMEM(stack, jnp.bfloat16),
            pltpu.VMEM((t1,) + stack, jnp.bfloat16),
            pltpu.VMEM((r1,) + stack, jnp.bfloat16),
            pltpu.VMEM((r1, rows, LANES), jnp.int32),
            pltpu.VMEM((tensor_size, local * pieces, LANES), jnp.bfloat16),
            pltpu.VMEM(down.shape, jnp.bfloat16),
            pltpu.VMEM(up.shape, jnp.bfloat16),
            pltpu.VMEM((tensor_size, 2 * band, local * pieces // 2), jnp.bfloat16),
            pltpu.VMEM((2 * band, 2 * LANES), jnp.float32),
            pltpu.VMEM((group_rows, LANES), jnp.float32),
            pltpu.VMEM((t1, group_rows, LANES), jnp.float32),
            pltpu.VMEM((replica_size, band, LANES), jnp.float32),
            pltpu.VMEM((r1, band, LANES), jnp.float32),
            pltpu.SemaphoreType.DMA((6 + tensor_size,)),
            pltpu.SemaphoreType.DMA((copies,)),
            pltpu.SemaphoreType.DMA((copies,)),
        ],
        compiler_params=pltpu.CompilerParams(
            collective_id=0, has_side_effects=True, vmem_limit_bytes=58 << 20
        ),
        cost_estimate=pl.CostEstimate(
            flops=2 * rows * width * pieces * LANES,
            bytes_accessed=2 * (weight.size + down.size + up.size),
            transcendentals=0,
        ),
    )(hidden, queries, lengths, ids, keys, values, weight, down, up)


def solution(mesh):
    in_specs = (
        P(("group", "replica"), "tensor"),
        P(("group", "replica"), "tensor", None),
        P(("group", "replica"), "tensor", None, None),
        P(("group", "replica"), "tensor", None, None),
        P(("group", "replica")),
        P(("group", "replica")),
        P(None, None, "tensor"),
        P(("group", "replica"), "tensor", None),
        P(("group", "replica"), None, None, "tensor"),
    )
    out_specs = P(("group", "replica"), "tensor")
    body = functools.partial(project, mesh.shape["tensor"], mesh.shape["replica"])
    return jax.shard_map(
        body, mesh=mesh, in_specs=in_specs, out_specs=out_specs, check_vma=False
    )
```

```python
import functools
import math

import jax
import jax.numpy as jnp
from jax import lax
from jax.experimental import pallas as pl
from jax.experimental.pallas import tpu as pltpu
from jax.sharding import PartitionSpec as P

adapter_scale = 2.0
LANES = 128


def rotate_keys(vectors, cosine, sine):
    half_size = vectors.shape[1] // 2
    lane = lax.broadcasted_iota(jnp.int32, vectors.shape, 1)
    swapped = pltpu.roll(vectors, half_size, 1)
    return vectors * cosine + jnp.where(lane < half_size, -swapped, swapped) * sine


def dot(a, b):
    return jnp.dot(a, b, preferred_element_type=jnp.float32)


def project_kernel(
    tensor_size, replica_size, pieces,
    h_ref, query_ref, lengths_ref, index_ref, key_hbm, value_hbm, weight_hbm, down_hbm, up_hbm,
    out_ref, ids_ref, keys, values, query32, mixed, peak, mass, hs_own, hs_t, hs_r, ids_r, weight, down, up, expanded, total,
    low_own, low_rx, delta_tx, delta_rx,
    load_sem, send_sem, recv_sem,
):
    rows, local = h_ref.shape
    blocks = local // LANES
    half_blocks = blocks // 2
    band = rows * pieces
    wide = LANES * pieces
    half_depth = half_blocks * wide
    shard_depth = 2 * half_depth
    rank2 = 32
    adapters = down.shape[0] // rank2
    per_tile = LANES // rank2
    tiles = adapters // per_tile

    me_t = lax.axis_index("tensor")
    me_r = lax.axis_index("replica")

    def t_at(step):
        return lax.rem(me_t + step + tensor_size, tensor_size)

    def r_at(step):
        return lax.rem(me_r + step + replica_size, replica_size)

    loads = [
        pltpu.make_async_copy(down_hbm, down, load_sem.at[0]),
        pltpu.make_async_copy(up_hbm, up, load_sem.at[1]),
    ]
    for d in range(tensor_size):
        source = pl.ds(pl.multiple_of(t_at(-d) * shard_depth, shard_depth), shard_depth)
        loads.append(
            pltpu.make_async_copy(weight_hbm.at[source], weight.at[d], load_sem.at[2 + d])
        )
    heads = keys.shape[1]
    row_half = rows // 2
    cache_loads = []
    for part in range(2):
        span = pl.ds(part * row_half, row_half)
        for source, target in ((key_hbm, keys), (value_hbm, values)):
            cache_loads.append(
                pltpu.make_async_copy(
                    source.at[span], target.at[span],
                    load_sem.at[2 + tensor_size + len(cache_loads)],
                )
            )
    for load in loads[2:3] + loads[:2] + cache_loads + loads[3:]:
        load.start()

    barrier = pltpu.get_barrier_semaphore()
    for d in range(1, tensor_size):
        pl.semaphore_signal(barrier, inc=1, device_id={"tensor": t_at(d)},
                            device_id_type=pl.DeviceIdType.MESH)
    for d in range(1, replica_size):
        pl.semaphore_signal(barrier, inc=1, device_id={"replica": r_at(d)},
                            device_id_type=pl.DeviceIdType.MESH)

    h32 = h_ref[...].astype(jnp.float32)
    hs_own[...] = jnp.concatenate(
        [h32[:, b * LANES:(b + 1) * LANES] for b in range(blocks)], axis=0
    ).astype(jnp.bfloat16)
    for r in range(rows):
        ids_ref[r:r + 1, :] = jnp.full((1, LANES), index_ref[r], jnp.int32)
    lane_of = lax.broadcasted_iota(jnp.int32, (rows, wide), 1)
    piece_shift = pieces.bit_length() - 1
    row_of = lax.broadcasted_iota(jnp.int32, (LANES, wide), 0)
    column_of = lax.broadcasted_iota(jnp.int32, (LANES, wide), 1)
    spread = jnp.where(
        lax.shift_right_logical(column_of, piece_shift) == row_of, 1.0, 0.0
    ).astype(jnp.bfloat16)
    piece_of = lane_of & (pieces - 1)

    def expand(source, d):
        repeated = dot(source, spread)
        for b in range(blocks):
            one = repeated[b * rows:(b + 1) * rows]
            parts = [jnp.where(piece_of == j, one, 0.0) for j in range(pieces)]
            half, at = divmod(b, half_blocks)
            expanded[d, half * band:(half + 1) * band, at * wide:(at + 1) * wide] = (
                jnp.concatenate(parts, axis=0).astype(jnp.bfloat16)
            )

    expand(hs_own[...], 0)
    total[...] = jnp.zeros_like(total)
    head_width = query_ref.shape[2]
    position = jnp.concatenate(
        [jnp.full((1, head_width), lengths_ref[r], jnp.int32) for r in range(rows)], axis=0
    ).astype(jnp.float32)
    lane = lax.broadcasted_iota(jnp.int32, (rows, head_width), 1) & (head_width // 2 - 1)
    frequency = jnp.exp(lane.astype(jnp.float32) * (-2.0 * math.log(500000.0) / head_width))
    cosine, sine = jnp.cos(position * frequency), jnp.sin(position * frequency)
    pl.semaphore_wait(barrier, tensor_size + replica_size - 2)

    count = [0]

    def remote(source, target, device):
        slot = count[0]
        count[0] += 1
        copy = pltpu.make_async_remote_copy(
            src_ref=source, dst_ref=target, send_sem=send_sem.at[slot],
            recv_sem=recv_sem.at[slot], device_id=device,
            device_id_type=pl.DeviceIdType.MESH,
        )
        copy.start()
        return copy

    ids_copies = [
        remote(ids_ref, ids_r.at[d - 1], {"replica": r_at(d)}) for d in range(1, replica_size)
    ]
    r_copies = [
        remote(hs_own, hs_r.at[d - 1], {"replica": r_at(d)}) for d in range(1, replica_size)
    ]
    t_copies = [
        remote(hs_own, hs_t.at[d - 1], {"tensor": t_at(d)}) for d in range(1, tensor_size)
    ]

    chunk = min(1024, half_depth)

    def accumulate(d):
        loads[2 + d].wait()

        def body(i, acc):
            at = pl.multiple_of(i * chunk, chunk)
            right = jnp.concatenate(
                [weight[d, pl.ds(at, chunk), :], weight[d, pl.ds(half_depth + at, chunk), :]],
                axis=1,
            )
            return acc + dot(expanded[d, :, pl.ds(at, chunk)], right)

        total[...] = lax.fori_loop(0, half_depth // chunk, body, total[...])

    group_size = query_ref.shape[1] // heads
    cache = keys.shape[2]
    scale = head_width ** (-0.5)

    def attend(r):
        query = query_ref[r].astype(jnp.float32)
        query32[r] = query
        if heads > 1:
            owner = lax.broadcasted_iota(jnp.int32, query.shape, 0)
            query = jnp.concatenate(
                [
                    jnp.where(
                        (owner >= c * group_size) & (owner < (c + 1) * group_size), query, 0.0
                    )
                    for c in range(heads)
                ],
                axis=1,
            )
        key_row = jnp.concatenate([keys[r, c] for c in range(heads)], axis=1)
        value_row = jnp.concatenate([values[r, c] for c in range(heads)], axis=1)
        scores = lax.dot_general(
            query.astype(jnp.bfloat16), key_row, (((1,), (1,)), ((), ())),
            preferred_element_type=jnp.float32,
        ) * scale
        position = lax.broadcasted_iota(jnp.int32, scores.shape, 1)
        scores = jnp.where(position < lengths_ref[r], scores, -1e30)
        top = jnp.max(scores, axis=1, keepdims=True)
        raw = jnp.exp(scores - top)
        both = dot(raw.astype(jnp.bfloat16), value_row)
        mixed[r] = jnp.concatenate(
            [
                both[c * group_size:(c + 1) * group_size, c * head_width:(c + 1) * head_width]
                for c in range(heads)
            ],
            axis=0,
        )
        wide_shape = (heads * group_size, head_width)
        peak[r] = jnp.broadcast_to(top, wide_shape)
        mass[r] = jnp.broadcast_to(jnp.sum(raw, axis=1, keepdims=True), wide_shape)


    accumulate(0)

    loads[0].wait()
    for copy in ids_copies + r_copies:
        copy.wait_recv()
    stacks = [hs_own[...].astype(jnp.float32)] + [
        hs_r[d - 1].astype(jnp.float32) for d in range(1, replica_size)
    ]
    all_rows = jnp.concatenate(
        [
            jnp.concatenate([s[b * rows:(b + 1) * rows] for s in stacks], axis=0).astype(
                jnp.bfloat16
            )
            for b in range(blocks)
        ],
        axis=1,
    )
    low_all = lax.dot_general(
        all_rows, down[...], (((1,), (1,)), ((), ())), preferred_element_type=jnp.float32
    )
    ids = jnp.concatenate(
        [ids_ref[...]] + [ids_r[d - 1] for d in range(1, replica_size)], axis=0
    ) - me_r * adapters
    lane = lax.broadcasted_iota(jnp.int32, ids.shape, 1)
    adapter_of = lax.shift_right_logical(lane, rank2.bit_length() - 1)
    chosen = [ids == adapter_of + k * per_tile for k in range(tiles)]
    low = jnp.zeros(ids.shape, jnp.float32)
    for k in range(tiles):
        low = low + jnp.where(chosen[k], low_all[:, k * LANES:(k + 1) * LANES], 0.0)
    quarter = lax.shift_right_logical(
        lax.broadcasted_iota(jnp.int32, (rows, LANES), 1), rank2.bit_length() - 1
    )

    def fill(x):
        full = x
        for turn in range(1, per_tile):
            full = full + pltpu.roll(x, turn * rank2, 1)
        return full

    filled = fill(low)
    packed = []
    for base in range(0, replica_size, per_tile):
        one = jnp.zeros((rows, LANES), jnp.float32)
        for g in range(per_tile):
            at = (base + g) * rows
            one = jnp.where(quarter == g, filled[at:at + rows], one)
        packed.append(one)
    low = jnp.concatenate(packed, axis=0)
    low_own[...] = low
    low_copies = [
        remote(low_own, low_rx.at[d - 1], {"tensor": t_at(d)}) for d in range(1, tensor_size)
    ]

    for part in range(2):
        for load in cache_loads[2 * part:2 * part + 2]:
            load.wait()
        for r in range(part * row_half, (part + 1) * row_half):
            attend(r)

    loads[1].wait()
    for copy in low_copies:
        copy.wait_recv()
    for d in range(1, tensor_size):
        low = low + low_rx[d - 1]
    unpacked = []
    for d in range(replica_size):
        at = (d // per_tile) * rows
        unpacked.append(jnp.where(quarter == d % per_tile, low[at:at + rows], 0.0))
    low = fill(jnp.concatenate(unpacked, axis=0))
    spread_low = jnp.concatenate([jnp.where(chosen[k], low, 0.0) for k in range(tiles)], axis=1)
    which = lax.broadcasted_iota(jnp.int32, spread_low.shape, 1) & (rank2 - 1)
    first = which < rank2 // 2
    left = jnp.concatenate(
        [jnp.where(first, spread_low, 0.0), jnp.where(first, 0.0, spread_low)], axis=0
    )
    top = left.astype(jnp.bfloat16)
    rest = left - top.astype(jnp.float32)
    middle = rest.astype(jnp.bfloat16)
    bottom = (rest - middle.astype(jnp.float32)).astype(jnp.bfloat16)
    delta = dot(top, up[...]) + (dot(middle, up[...]) + dot(bottom, up[...]))
    group_rows = rows * replica_size
    for d in range(replica_size):
        delta_tx[d] = jnp.concatenate(
            [
                delta[
                    (j % 2) * group_rows + d * rows:(j % 2) * group_rows + (d + 1) * rows,
                    (j // 2) * LANES:(j // 2 + 1) * LANES,
                ]
                for j in range(pieces)
            ],
            axis=0,
        )
    delta_copies = [
        remote(delta_tx.at[d], delta_rx.at[d - 1], {"replica": r_at(-d)})
        for d in range(1, replica_size)
    ]

    for d in range(1, tensor_size):
        t_copies[d - 1].wait_recv()
        expand(hs_t[d - 1], d)
        accumulate(d)

    result = total[0:band, 0:LANES] + total[band:2 * band, LANES:2 * LANES]
    update = delta_tx[0]
    for d in range(1, replica_size):
        delta_copies[d - 1].wait_recv()
        update = update + delta_rx[d - 1]
    projected = result + adapter_scale * update

    outputs = []
    for c in range(heads):
        at = 2 * c * rows
        new_key = rotate_keys(projected[at:at + rows], cosine, sine)
        new_key = new_key.astype(jnp.bfloat16).astype(jnp.float32)
        new_value = projected[at + rows:at + 2 * rows].astype(jnp.bfloat16).astype(jnp.float32)
        for h in range(c * group_size, (c + 1) * group_size):
            fresh = jnp.sum(query32[:, h, :] * new_key, axis=1, keepdims=True) * scale
            old_peak = peak[:, h, :]
            new_peak = jnp.maximum(old_peak, fresh)
            keep = jnp.exp(old_peak - new_peak)
            fresh_raw = jnp.exp(fresh - new_peak)
            outputs.append(
                (mixed[:, h, :] * keep + fresh_raw * new_value)
                / (mass[:, h, :] * keep + fresh_raw)
            )
    out_ref[...] = jnp.concatenate(outputs, axis=1).astype(out_ref.dtype)
    for copy in ids_copies + r_copies + t_copies + low_copies + delta_copies:
        copy.wait_send()


def project(tensor_size, replica_size, hidden, queries, keys, values, lengths, ids, weight, down, up):
    rows, local = hidden.shape
    width = weight.shape[0]
    pieces = weight.shape[1] * weight.shape[2] // LANES
    blocks = local // LANES
    band = rows * pieces
    weight = (
        weight.reshape(width, 2, pieces // 2, LANES)
        .transpose(0, 2, 1, 3)
        .reshape(width * pieces, LANES)
    )
    adapters, _, rank2 = down.shape
    down = down.transpose(0, 2, 1).reshape(adapters * rank2, local)
    up = up.reshape(adapters * rank2, up.shape[3])
    t1, r1 = tensor_size - 1, replica_size - 1
    copies = 2 * t1 + 3 * r1
    vmem = pl.BlockSpec(memory_space=pltpu.VMEM)
    smem = pl.BlockSpec(memory_space=pltpu.SMEM)
    hbm = pl.BlockSpec(memory_space=pl.ANY)
    stack = (blocks * rows, LANES)
    group_rows = rows * replica_size * 32 // LANES
    return pl.pallas_call(
        functools.partial(project_kernel, tensor_size, replica_size, pieces),
        out_shape=jax.ShapeDtypeStruct(
            (rows, queries.shape[1] * queries.shape[2]), jnp.float32
        ),
        in_specs=[vmem, vmem, smem, smem, hbm, hbm, hbm, hbm, hbm],
        out_specs=vmem,
        scratch_shapes=[
            pltpu.VMEM((rows, LANES), jnp.int32),
            pltpu.VMEM(keys.shape, jnp.bfloat16),
            pltpu.VMEM(values.shape, jnp.bfloat16),
            pltpu.VMEM(queries.shape, jnp.float32),
            pltpu.VMEM(queries.shape, jnp.float32),
            pltpu.VMEM(queries.shape, jnp.float32),
            pltpu.VMEM(queries.shape, jnp.float32),
            pltpu.VMEM(stack, jnp.bfloat16),
            pltpu.VMEM((t1,) + stack, jnp.bfloat16),
            pltpu.VMEM((r1,) + stack, jnp.bfloat16),
            pltpu.VMEM((r1, rows, LANES), jnp.int32),
            pltpu.VMEM((tensor_size, local * pieces, LANES), jnp.bfloat16),
            pltpu.VMEM(down.shape, jnp.bfloat16),
            pltpu.VMEM(up.shape, jnp.bfloat16),
            pltpu.VMEM((tensor_size, 2 * band, local * pieces // 2), jnp.bfloat16),
            pltpu.VMEM((2 * band, 2 * LANES), jnp.float32),
            pltpu.VMEM((group_rows, LANES), jnp.float32),
            pltpu.VMEM((t1, group_rows, LANES), jnp.float32),
            pltpu.VMEM((replica_size, band, LANES), jnp.float32),
            pltpu.VMEM((r1, band, LANES), jnp.float32),
            pltpu.SemaphoreType.DMA((6 + tensor_size,)),
            pltpu.SemaphoreType.DMA((copies,)),
            pltpu.SemaphoreType.DMA((copies,)),
        ],
        compiler_params=pltpu.CompilerParams(
            collective_id=0, has_side_effects=True, vmem_limit_bytes=58 << 20
        ),
        cost_estimate=pl.CostEstimate(
            flops=2 * rows * width * pieces * LANES,
            bytes_accessed=2 * (weight.size + down.size + up.size),
            transcendentals=0,
        ),
    )(hidden, queries, lengths, ids, keys, values, weight, down, up).astype(jnp.bfloat16)


def solution(mesh):
    in_specs = (
        P(("group", "replica"), "tensor"),
        P(("group", "replica"), "tensor", None),
        P(("group", "replica"), "tensor", None, None),
        P(("group", "replica"), "tensor", None, None),
        P(("group", "replica")),
        P(("group", "replica")),
        P(None, None, "tensor"),
        P(("group", "replica"), "tensor", None),
        P(("group", "replica"), None, None, "tensor"),
    )
    out_specs = P(("group", "replica"), "tensor")
    body = functools.partial(project, mesh.shape["tensor"], mesh.shape["replica"])
    return jax.shard_map(
        body, mesh=mesh, in_specs=in_specs, out_specs=out_specs, check_vma=False
    )
```

```python
import functools
import math

import jax
import jax.numpy as jnp
from jax import lax
from jax.experimental import pallas as pl
from jax.experimental.pallas import tpu as pltpu
from jax.sharding import PartitionSpec as P

adapter_scale = 2.0
LANES = 128


def rotate_keys(vectors, cosine, sine):
    half_size = vectors.shape[1] // 2
    lane = lax.broadcasted_iota(jnp.int32, vectors.shape, 1)
    swapped = pltpu.roll(vectors, half_size, 1)
    return vectors * cosine + jnp.where(lane < half_size, -swapped, swapped) * sine


def dot(a, b):
    return jnp.dot(a, b, preferred_element_type=jnp.float32)


def project_kernel(
    tensor_size, replica_size, pieces,
    h_ref, query_ref, lengths_ref, index_ref, key_hbm, value_hbm, weight_hbm, down_hbm, up_hbm,
    out_ref, ids_ref, keys, values, query32, mixed, peak, mass, hs_own, hs_t, hs_r, ids_r, weight, down, up, expanded, total,
    low_own, low_rx, delta_tx, delta_rx,
    load_sem, send_sem, recv_sem,
):
    rows, local = h_ref.shape
    blocks = local // LANES
    half_blocks = blocks // 2
    band = rows * pieces
    wide = LANES * pieces
    half_depth = half_blocks * wide
    shard_depth = 2 * half_depth
    rank2 = 32
    adapters = down.shape[0] // rank2
    per_tile = LANES // rank2
    tiles = adapters // per_tile

    me_t = lax.axis_index("tensor")
    me_r = lax.axis_index("replica")

    def t_at(step):
        return lax.rem(me_t + step + tensor_size, tensor_size)

    def r_at(step):
        return lax.rem(me_r + step + replica_size, replica_size)

    barrier = pltpu.get_barrier_semaphore()
    for d in range(1, tensor_size):
        pl.semaphore_signal(barrier, inc=1, device_id={"tensor": t_at(d)},
                            device_id_type=pl.DeviceIdType.MESH)
    for d in range(1, replica_size):
        pl.semaphore_signal(barrier, inc=1, device_id={"replica": r_at(d)},
                            device_id_type=pl.DeviceIdType.MESH)

    loads = [
        pltpu.make_async_copy(down_hbm, down, load_sem.at[0]),
        pltpu.make_async_copy(up_hbm, up, load_sem.at[1]),
    ]
    for d in range(tensor_size):
        source = pl.ds(pl.multiple_of(t_at(-d) * shard_depth, shard_depth), shard_depth)
        loads.append(
            pltpu.make_async_copy(weight_hbm.at[source], weight.at[d], load_sem.at[2 + d])
        )
    heads = keys.shape[1]
    row_half = rows // 2
    cache_loads = []
    for part in range(2):
        span = pl.ds(part * row_half, row_half)
        for source, target in ((key_hbm, keys), (value_hbm, values)):
            cache_loads.append(
                pltpu.make_async_copy(
                    source.at[span], target.at[span],
                    load_sem.at[2 + tensor_size + len(cache_loads)],
                )
            )
    for load in loads[2:3] + loads[:2] + cache_loads + loads[3:]:
        load.start()

    h32 = h_ref[...].astype(jnp.float32)
    hs_own[...] = jnp.concatenate(
        [h32[:, b * LANES:(b + 1) * LANES] for b in range(blocks)], axis=0
    ).astype(jnp.bfloat16)
    for r in range(rows):
        ids_ref[r:r + 1, :] = jnp.full((1, LANES), index_ref[r], jnp.int32)
    pl.semaphore_wait(barrier, tensor_size + replica_size - 2)

    count = [0]

    def remote(source, target, device):
        slot = count[0]
        count[0] += 1
        copy = pltpu.make_async_remote_copy(
            src_ref=source, dst_ref=target, send_sem=send_sem.at[slot],
            recv_sem=recv_sem.at[slot], device_id=device,
            device_id_type=pl.DeviceIdType.MESH,
        )
        copy.start()
        return copy

    ids_copies = [
        remote(ids_ref, ids_r.at[d - 1], {"replica": r_at(d)}) for d in range(1, replica_size)
    ]
    r_copies = [
        remote(hs_own, hs_r.at[d - 1], {"replica": r_at(d)}) for d in range(1, replica_size)
    ]

    lane_of = lax.broadcasted_iota(jnp.int32, (rows, wide), 1)
    piece_shift = pieces.bit_length() - 1
    row_of = lax.broadcasted_iota(jnp.int32, (LANES, wide), 0)
    column_of = lax.broadcasted_iota(jnp.int32, (LANES, wide), 1)
    spread = jnp.where(
        lax.shift_right_logical(column_of, piece_shift) == row_of, 1.0, 0.0
    ).astype(jnp.bfloat16)
    piece_of = lane_of & (pieces - 1)

    def expand(source, d):
        repeated = dot(source, spread)
        for b in range(blocks):
            one = repeated[b * rows:(b + 1) * rows]
            parts = [jnp.where(piece_of == j, one, 0.0) for j in range(pieces)]
            half, at = divmod(b, half_blocks)
            expanded[d, half * band:(half + 1) * band, at * wide:(at + 1) * wide] = (
                jnp.concatenate(parts, axis=0).astype(jnp.bfloat16)
            )

    expand(hs_own[...], 0)
    total[...] = jnp.zeros_like(total)
    head_width = query_ref.shape[2]
    position = jnp.concatenate(
        [jnp.full((1, head_width), lengths_ref[r], jnp.int32) for r in range(rows)], axis=0
    ).astype(jnp.float32)
    lane = lax.broadcasted_iota(jnp.int32, (rows, head_width), 1) & (head_width // 2 - 1)
    frequency = jnp.exp(lane.astype(jnp.float32) * (-2.0 * math.log(500000.0) / head_width))
    cosine, sine = jnp.cos(position * frequency), jnp.sin(position * frequency)
    chunk = min(1024, half_depth)

    def accumulate(d):
        loads[2 + d].wait()

        def body(i, acc):
            at = pl.multiple_of(i * chunk, chunk)
            right = jnp.concatenate(
                [weight[d, pl.ds(at, chunk), :], weight[d, pl.ds(half_depth + at, chunk), :]],
                axis=1,
            )
            return acc + dot(expanded[d, :, pl.ds(at, chunk)], right)

        total[...] = lax.fori_loop(0, half_depth // chunk, body, total[...])

    group_size = query_ref.shape[1] // heads
    cache = keys.shape[2]
    scale = head_width ** (-0.5)

    def attend(r):
        query = query_ref[r].astype(jnp.float32)
        query32[r] = query
        if heads > 1:
            owner = lax.broadcasted_iota(jnp.int32, query.shape, 0)
            query = jnp.concatenate(
                [
                    jnp.where(
                        (owner >= c * group_size) & (owner < (c + 1) * group_size), query, 0.0
                    )
                    for c in range(heads)
                ],
                axis=1,
            )
        key_row = jnp.concatenate([keys[r, c] for c in range(heads)], axis=1)
        value_row = jnp.concatenate([values[r, c] for c in range(heads)], axis=1)
        scores = lax.dot_general(
            query.astype(jnp.bfloat16), key_row, (((1,), (1,)), ((), ())),
            preferred_element_type=jnp.float32,
        ) * scale
        position = lax.broadcasted_iota(jnp.int32, scores.shape, 1)
        scores = jnp.where(position < lengths_ref[r], scores, -1e30)
        top = jnp.max(scores, axis=1, keepdims=True)
        raw = jnp.exp(scores - top)
        both = dot(raw.astype(jnp.bfloat16), value_row)
        mixed[r] = jnp.concatenate(
            [
                both[c * group_size:(c + 1) * group_size, c * head_width:(c + 1) * head_width]
                for c in range(heads)
            ],
            axis=0,
        )
        wide_shape = (heads * group_size, head_width)
        peak[r] = jnp.broadcast_to(top, wide_shape)
        mass[r] = jnp.broadcast_to(jnp.sum(raw, axis=1, keepdims=True), wide_shape)


    accumulate(0)

    loads[0].wait()
    for copy in ids_copies + r_copies:
        copy.wait_recv()
    stacks = [hs_own[...].astype(jnp.float32)] + [
        hs_r[d - 1].astype(jnp.float32) for d in range(1, replica_size)
    ]
    all_rows = jnp.concatenate(
        [
            jnp.concatenate([s[b * rows:(b + 1) * rows] for s in stacks], axis=0).astype(
                jnp.bfloat16
            )
            for b in range(blocks)
        ],
        axis=1,
    )
    low_all = lax.dot_general(
        all_rows, down[...], (((1,), (1,)), ((), ())), preferred_element_type=jnp.float32
    )
    ids = jnp.concatenate(
        [ids_ref[...]] + [ids_r[d - 1] for d in range(1, replica_size)], axis=0
    ) - me_r * adapters
    lane = lax.broadcasted_iota(jnp.int32, ids.shape, 1)
    adapter_of = lax.shift_right_logical(lane, rank2.bit_length() - 1)
    chosen = [ids == adapter_of + k * per_tile for k in range(tiles)]
    low = jnp.zeros(ids.shape, jnp.float32)
    for k in range(tiles):
        low = low + jnp.where(chosen[k], low_all[:, k * LANES:(k + 1) * LANES], 0.0)
    quarter = lax.shift_right_logical(
        lax.broadcasted_iota(jnp.int32, (rows, LANES), 1), rank2.bit_length() - 1
    )

    def fill(x):
        full = x
        for turn in range(1, per_tile):
            full = full + pltpu.roll(x, turn * rank2, 1)
        return full

    filled = fill(low)
    packed = []
    for base in range(0, replica_size, per_tile):
        one = jnp.zeros((rows, LANES), jnp.float32)
        for g in range(per_tile):
            at = (base + g) * rows
            one = jnp.where(quarter == g, filled[at:at + rows], one)
        packed.append(one)
    low = jnp.concatenate(packed, axis=0)
    low_own[...] = low
    low_copies = [
        remote(low_own, low_rx.at[d - 1], {"tensor": t_at(d)}) for d in range(1, tensor_size)
    ]
    t_copies = [
        remote(hs_own, hs_t.at[d - 1], {"tensor": t_at(d)}) for d in range(1, tensor_size)
    ]

    for part in range(2):
        for load in cache_loads[2 * part:2 * part + 2]:
            load.wait()
        for r in range(part * row_half, (part + 1) * row_half):
            attend(r)

    loads[1].wait()
    for copy in low_copies:
        copy.wait_recv()
    for d in range(1, tensor_size):
        low = low + low_rx[d - 1]
    unpacked = []
    for d in range(replica_size):
        at = (d // per_tile) * rows
        unpacked.append(jnp.where(quarter == d % per_tile, low[at:at + rows], 0.0))
    low = fill(jnp.concatenate(unpacked, axis=0))
    spread_low = jnp.concatenate([jnp.where(chosen[k], low, 0.0) for k in range(tiles)], axis=1)
    which = lax.broadcasted_iota(jnp.int32, spread_low.shape, 1) & (rank2 - 1)
    first = which < rank2 // 2
    left = jnp.concatenate(
        [jnp.where(first, spread_low, 0.0), jnp.where(first, 0.0, spread_low)], axis=0
    )
    top = left.astype(jnp.bfloat16)
    rest = left - top.astype(jnp.float32)
    middle = rest.astype(jnp.bfloat16)
    bottom = (rest - middle.astype(jnp.float32)).astype(jnp.bfloat16)
    delta = dot(top, up[...]) + (dot(middle, up[...]) + dot(bottom, up[...]))
    group_rows = rows * replica_size
    for d in range(replica_size):
        delta_tx[d] = jnp.concatenate(
            [
                delta[
                    (j % 2) * group_rows + d * rows:(j % 2) * group_rows + (d + 1) * rows,
                    (j // 2) * LANES:(j // 2 + 1) * LANES,
                ]
                for j in range(pieces)
            ],
            axis=0,
        )
    delta_copies = [
        remote(delta_tx.at[d], delta_rx.at[d - 1], {"replica": r_at(-d)})
        for d in range(1, replica_size)
    ]

    for d in range(1, tensor_size):
        t_copies[d - 1].wait_recv()
        expand(hs_t[d - 1], d)
        accumulate(d)

    result = total[0:band, 0:LANES] + total[band:2 * band, LANES:2 * LANES]
    update = delta_tx[0]
    for d in range(1, replica_size):
        delta_copies[d - 1].wait_recv()
        update = update + delta_rx[d - 1]
    projected = result + adapter_scale * update

    outputs = []
    for c in range(heads):
        at = 2 * c * rows
        new_key = rotate_keys(projected[at:at + rows], cosine, sine)
        new_key = new_key.astype(jnp.bfloat16).astype(jnp.float32)
        new_value = projected[at + rows:at + 2 * rows].astype(jnp.bfloat16).astype(jnp.float32)
        for h in range(c * group_size, (c + 1) * group_size):
            fresh = jnp.sum(query32[:, h, :] * new_key, axis=1, keepdims=True) * scale
            old_peak = peak[:, h, :]
            new_peak = jnp.maximum(old_peak, fresh)
            keep = jnp.exp(old_peak - new_peak)
            fresh_raw = jnp.exp(fresh - new_peak)
            outputs.append(
                (mixed[:, h, :] * keep + fresh_raw * new_value)
                / (mass[:, h, :] * keep + fresh_raw)
            )
    out_ref[...] = jnp.concatenate(outputs, axis=1).astype(out_ref.dtype)
    for copy in ids_copies + r_copies + t_copies + low_copies + delta_copies:
        copy.wait_send()


def project(tensor_size, replica_size, hidden, queries, keys, values, lengths, ids, weight, down, up):
    rows, local = hidden.shape
    width = weight.shape[0]
    pieces = weight.shape[1] * weight.shape[2] // LANES
    blocks = local // LANES
    band = rows * pieces
    weight = (
        weight.reshape(width, 2, pieces // 2, LANES)
        .transpose(0, 2, 1, 3)
        .reshape(width * pieces, LANES)
    )
    adapters, _, rank2 = down.shape
    down = down.transpose(0, 2, 1).reshape(adapters * rank2, local)
    up = up.reshape(adapters * rank2, up.shape[3])
    t1, r1 = tensor_size - 1, replica_size - 1
    copies = 2 * t1 + 3 * r1
    vmem = pl.BlockSpec(memory_space=pltpu.VMEM)
    smem = pl.BlockSpec(memory_space=pltpu.SMEM)
    hbm = pl.BlockSpec(memory_space=pl.ANY)
    stack = (blocks * rows, LANES)
    group_rows = rows * replica_size * 32 // LANES
    return pl.pallas_call(
        functools.partial(project_kernel, tensor_size, replica_size, pieces),
        out_shape=jax.ShapeDtypeStruct(
            (rows, queries.shape[1] * queries.shape[2]), jnp.bfloat16
        ),
        in_specs=[vmem, vmem, smem, smem, hbm, hbm, hbm, hbm, hbm],
        out_specs=vmem,
        scratch_shapes=[
            pltpu.VMEM((rows, LANES), jnp.int32),
            pltpu.VMEM(keys.shape, jnp.bfloat16),
            pltpu.VMEM(values.shape, jnp.bfloat16),
            pltpu.VMEM(queries.shape, jnp.float32),
            pltpu.VMEM(queries.shape, jnp.float32),
            pltpu.VMEM(queries.shape, jnp.float32),
            pltpu.VMEM(queries.shape, jnp.float32),
            pltpu.VMEM(stack, jnp.bfloat16),
            pltpu.VMEM((t1,) + stack, jnp.bfloat16),
            pltpu.VMEM((r1,) + stack, jnp.bfloat16),
            pltpu.VMEM((r1, rows, LANES), jnp.int32),
            pltpu.VMEM((tensor_size, local * pieces, LANES), jnp.bfloat16),
            pltpu.VMEM(down.shape, jnp.bfloat16),
            pltpu.VMEM(up.shape, jnp.bfloat16),
            pltpu.VMEM((tensor_size, 2 * band, local * pieces // 2), jnp.bfloat16),
            pltpu.VMEM((2 * band, 2 * LANES), jnp.float32),
            pltpu.VMEM((group_rows, LANES), jnp.float32),
            pltpu.VMEM((t1, group_rows, LANES), jnp.float32),
            pltpu.VMEM((replica_size, band, LANES), jnp.float32),
            pltpu.VMEM((r1, band, LANES), jnp.float32),
            pltpu.SemaphoreType.DMA((6 + tensor_size,)),
            pltpu.SemaphoreType.DMA((copies,)),
            pltpu.SemaphoreType.DMA((copies,)),
        ],
        compiler_params=pltpu.CompilerParams(
            collective_id=0, has_side_effects=True, vmem_limit_bytes=58 << 20
        ),
        cost_estimate=pl.CostEstimate(
            flops=2 * rows * width * pieces * LANES,
            bytes_accessed=2 * (weight.size + down.size + up.size),
            transcendentals=0,
        ),
    )(hidden, queries, lengths, ids, keys, values, weight, down, up)


def solution(mesh):
    in_specs = (
        P(("group", "replica"), "tensor"),
        P(("group", "replica"), "tensor", None),
        P(("group", "replica"), "tensor", None, None),
        P(("group", "replica"), "tensor", None, None),
        P(("group", "replica")),
        P(("group", "replica")),
        P(None, None, "tensor"),
        P(("group", "replica"), "tensor", None),
        P(("group", "replica"), None, None, "tensor"),
    )
    out_specs = P(("group", "replica"), "tensor")
    body = functools.partial(project, mesh.shape["tensor"], mesh.shape["replica"])
    return jax.shard_map(
        body, mesh=mesh, in_specs=in_specs, out_specs=out_specs, check_vma=False
    )
```

```python
import functools
import math

import jax
import jax.numpy as jnp
from jax import lax
from jax.experimental import pallas as pl
from jax.experimental.pallas import tpu as pltpu
from jax.sharding import PartitionSpec as P

adapter_scale = 2.0
LANES = 128


def rotate_keys(vectors, cosine, sine):
    half_size = vectors.shape[1] // 2
    lane = lax.broadcasted_iota(jnp.int32, vectors.shape, 1)
    swapped = pltpu.roll(vectors, half_size, 1)
    return vectors * cosine + jnp.where(lane < half_size, -swapped, swapped) * sine


def dot(a, b):
    return jnp.dot(a, b, preferred_element_type=jnp.float32)


def project_kernel(
    tensor_size, replica_size, pieces,
    h_ref, query_ref, lengths_ref, index_ref, key_hbm, value_hbm, weight_hbm, down_hbm, up_hbm,
    out_ref, ids_ref, keys, values, query32, mixed, peak, mass, hs_own, hs_t, hs_r, ids_r, weight, down, up, expanded, total,
    low_own, low_rx, delta_tx, delta_rx,
    load_sem, send_sem, recv_sem,
):
    rows, local = h_ref.shape
    blocks = local // LANES
    half_blocks = blocks // 2
    band = rows * pieces
    wide = LANES * pieces
    half_depth = half_blocks * wide
    shard_depth = 2 * half_depth
    rank2 = 32
    adapters = down.shape[0] // rank2
    per_tile = LANES // rank2
    tiles = adapters // per_tile

    me_t = lax.axis_index("tensor")
    me_r = lax.axis_index("replica")

    def t_at(step):
        return lax.rem(me_t + step + tensor_size, tensor_size)

    def r_at(step):
        return lax.rem(me_r + step + replica_size, replica_size)

    barrier = pltpu.get_barrier_semaphore()
    for d in range(1, tensor_size):
        pl.semaphore_signal(barrier, inc=1, device_id={"tensor": t_at(d)},
                            device_id_type=pl.DeviceIdType.MESH)
    for d in range(1, replica_size):
        pl.semaphore_signal(barrier, inc=1, device_id={"replica": r_at(d)},
                            device_id_type=pl.DeviceIdType.MESH)

    loads = [
        pltpu.make_async_copy(down_hbm, down, load_sem.at[0]),
        pltpu.make_async_copy(up_hbm, up, load_sem.at[1]),
    ]
    for d in range(tensor_size):
        source = pl.ds(pl.multiple_of(t_at(-d) * shard_depth, shard_depth), shard_depth)
        loads.append(
            pltpu.make_async_copy(weight_hbm.at[source], weight.at[d], load_sem.at[2 + d])
        )
    heads = keys.shape[1]
    row_half = rows // 2
    cache_loads = []
    for part in range(2):
        span = pl.ds(part * row_half, row_half)
        for source, target in ((key_hbm, keys), (value_hbm, values)):
            cache_loads.append(
                pltpu.make_async_copy(
                    source.at[span], target.at[span],
                    load_sem.at[2 + tensor_size + len(cache_loads)],
                )
            )
    for load in loads[2:3] + loads[:2] + cache_loads + loads[3:]:
        load.start()

    h32 = h_ref[...].astype(jnp.float32)
    hs_own[...] = jnp.concatenate(
        [h32[:, b * LANES:(b + 1) * LANES] for b in range(blocks)], axis=0
    ).astype(jnp.bfloat16)
    for r in range(rows):
        ids_ref[r:r + 1, :] = jnp.full((1, LANES), index_ref[r], jnp.int32)
    pl.semaphore_wait(barrier, tensor_size + replica_size - 2)

    count = [0]

    def remote(source, target, device):
        slot = count[0]
        count[0] += 1
        copy = pltpu.make_async_remote_copy(
            src_ref=source, dst_ref=target, send_sem=send_sem.at[slot],
            recv_sem=recv_sem.at[slot], device_id=device,
            device_id_type=pl.DeviceIdType.MESH,
        )
        copy.start()
        return copy

    ids_copies = [
        remote(ids_ref, ids_r.at[d - 1], {"replica": r_at(d)}) for d in range(1, replica_size)
    ]
    r_copies = [
        remote(hs_own, hs_r.at[d - 1], {"replica": r_at(d)}) for d in range(1, replica_size)
    ]

    lane_of = lax.broadcasted_iota(jnp.int32, (rows, wide), 1)
    piece_shift = pieces.bit_length() - 1
    row_of = lax.broadcasted_iota(jnp.int32, (LANES, wide), 0)
    column_of = lax.broadcasted_iota(jnp.int32, (LANES, wide), 1)
    spread = jnp.where(
        lax.shift_right_logical(column_of, piece_shift) == row_of, 1.0, 0.0
    ).astype(jnp.bfloat16)
    piece_of = lane_of & (pieces - 1)

    def expand(source, d):
        repeated = dot(source, spread)
        for b in range(blocks):
            one = repeated[b * rows:(b + 1) * rows]
            parts = [jnp.where(piece_of == j, one, 0.0) for j in range(pieces)]
            half, at = divmod(b, half_blocks)
            expanded[d, half * band:(half + 1) * band, at * wide:(at + 1) * wide] = (
                jnp.concatenate(parts, axis=0).astype(jnp.bfloat16)
            )

    expand(hs_own[...], 0)
    total[...] = jnp.zeros_like(total)
    head_width = query_ref.shape[2]
    position = jnp.concatenate(
        [jnp.full((1, head_width), lengths_ref[r], jnp.int32) for r in range(rows)], axis=0
    ).astype(jnp.float32)
    lane = lax.broadcasted_iota(jnp.int32, (rows, head_width), 1) & (head_width // 2 - 1)
    frequency = jnp.exp(lane.astype(jnp.float32) * (-2.0 * math.log(500000.0) / head_width))
    cosine, sine = jnp.cos(position * frequency), jnp.sin(position * frequency)
    chunk = min(1024, half_depth)

    def accumulate(d):
        loads[2 + d].wait()

        def body(i, acc):
            at = pl.multiple_of(i * chunk, chunk)
            right = jnp.concatenate(
                [weight[d, pl.ds(at, chunk), :], weight[d, pl.ds(half_depth + at, chunk), :]],
                axis=1,
            )
            return acc + dot(expanded[d, :, pl.ds(at, chunk)], right)

        total[...] = lax.fori_loop(0, half_depth // chunk, body, total[...])

    group_size = query_ref.shape[1] // heads
    cache = keys.shape[2]
    scale = head_width ** (-0.5)

    def attend(r):
        query = query_ref[r].astype(jnp.float32)
        query32[r] = query
        if heads > 1:
            owner = lax.broadcasted_iota(jnp.int32, query.shape, 0)
            query = jnp.concatenate(
                [
                    jnp.where(
                        (owner >= c * group_size) & (owner < (c + 1) * group_size), query, 0.0
                    )
                    for c in range(heads)
                ],
                axis=1,
            )
        key_row = jnp.concatenate([keys[r, c] for c in range(heads)], axis=1)
        value_row = jnp.concatenate([values[r, c] for c in range(heads)], axis=1)
        scores = lax.dot_general(
            query.astype(jnp.bfloat16), key_row, (((1,), (1,)), ((), ())),
            preferred_element_type=jnp.float32,
        ) * scale
        position = lax.broadcasted_iota(jnp.int32, scores.shape, 1)
        scores = jnp.where(position < lengths_ref[r], scores, -1e30)
        top = jnp.max(scores, axis=1, keepdims=True)
        raw = jnp.exp(scores - top)
        both = dot(raw.astype(jnp.bfloat16), value_row)
        mixed[r] = jnp.concatenate(
            [
                both[c * group_size:(c + 1) * group_size, c * head_width:(c + 1) * head_width]
                for c in range(heads)
            ],
            axis=0,
        )
        wide_shape = (heads * group_size, head_width)
        peak[r] = jnp.broadcast_to(top, wide_shape)
        mass[r] = jnp.broadcast_to(jnp.sum(raw, axis=1, keepdims=True), wide_shape)


    accumulate(0)

    loads[0].wait()
    for copy in ids_copies + r_copies:
        copy.wait_recv()
    stacks = [hs_own[...].astype(jnp.float32)] + [
        hs_r[d - 1].astype(jnp.float32) for d in range(1, replica_size)
    ]
    all_rows = jnp.concatenate(
        [
            jnp.concatenate([s[b * rows:(b + 1) * rows] for s in stacks], axis=0).astype(
                jnp.bfloat16
            )
            for b in range(blocks)
        ],
        axis=1,
    )
    low_all = lax.dot_general(
        all_rows, down[...], (((1,), (1,)), ((), ())), preferred_element_type=jnp.float32
    )
    ids = jnp.concatenate(
        [ids_ref[...]] + [ids_r[d - 1] for d in range(1, replica_size)], axis=0
    ) - me_r * adapters
    lane = lax.broadcasted_iota(jnp.int32, ids.shape, 1)
    adapter_of = lax.shift_right_logical(lane, rank2.bit_length() - 1)
    chosen = [ids == adapter_of + k * per_tile for k in range(tiles)]
    low = jnp.zeros(ids.shape, jnp.float32)
    for k in range(tiles):
        low = low + jnp.where(chosen[k], low_all[:, k * LANES:(k + 1) * LANES], 0.0)
    quarter = lax.shift_right_logical(
        lax.broadcasted_iota(jnp.int32, (rows, LANES), 1), rank2.bit_length() - 1
    )

    def fill(x):
        full = x
        for turn in range(1, per_tile):
            full = full + pltpu.roll(x, turn * rank2, 1)
        return full

    filled = fill(low)
    packed = []
    for base in range(0, replica_size, per_tile):
        one = jnp.zeros((rows, LANES), jnp.float32)
        for g in range(per_tile):
            at = (base + g) * rows
            one = jnp.where(quarter == g, filled[at:at + rows], one)
        packed.append(one)
    low = jnp.concatenate(packed, axis=0)
    low_own[...] = low
    low_copies = [
        remote(low_own, low_rx.at[d - 1], {"tensor": t_at(d)}) for d in range(1, tensor_size)
    ]
    t_copies = [
        remote(hs_own, hs_t.at[d - 1], {"tensor": t_at(d)}) for d in range(1, tensor_size)
    ]

    def attend_half(part):
        for load in cache_loads[2 * part:2 * part + 2]:
            load.wait()
        for r in range(part * row_half, (part + 1) * row_half):
            attend(r)

    attend_half(0)

    loads[1].wait()
    for copy in low_copies:
        copy.wait_recv()
    for d in range(1, tensor_size):
        low = low + low_rx[d - 1]
    unpacked = []
    for d in range(replica_size):
        at = (d // per_tile) * rows
        unpacked.append(jnp.where(quarter == d % per_tile, low[at:at + rows], 0.0))
    low = fill(jnp.concatenate(unpacked, axis=0))
    spread_low = jnp.concatenate([jnp.where(chosen[k], low, 0.0) for k in range(tiles)], axis=1)
    which = lax.broadcasted_iota(jnp.int32, spread_low.shape, 1) & (rank2 - 1)
    first = which < rank2 // 2
    left = jnp.concatenate(
        [jnp.where(first, spread_low, 0.0), jnp.where(first, 0.0, spread_low)], axis=0
    )
    top = left.astype(jnp.bfloat16)
    rest = left - top.astype(jnp.float32)
    middle = rest.astype(jnp.bfloat16)
    bottom = (rest - middle.astype(jnp.float32)).astype(jnp.bfloat16)
    delta = dot(top, up[...]) + (dot(middle, up[...]) + dot(bottom, up[...]))
    group_rows = rows * replica_size
    for d in range(replica_size):
        delta_tx[d] = jnp.concatenate(
            [
                delta[
                    (j % 2) * group_rows + d * rows:(j % 2) * group_rows + (d + 1) * rows,
                    (j // 2) * LANES:(j // 2 + 1) * LANES,
                ]
                for j in range(pieces)
            ],
            axis=0,
        )
    delta_copies = [
        remote(delta_tx.at[d], delta_rx.at[d - 1], {"replica": r_at(-d)})
        for d in range(1, replica_size)
    ]

    attend_half(1)
    for d in range(1, tensor_size):
        t_copies[d - 1].wait_recv()
        expand(hs_t[d - 1], d)
        accumulate(d)

    result = total[0:band, 0:LANES] + total[band:2 * band, LANES:2 * LANES]
    update = delta_tx[0]
    for d in range(1, replica_size):
        delta_copies[d - 1].wait_recv()
        update = update + delta_rx[d - 1]
    projected = result + adapter_scale * update

    outputs = []
    for c in range(heads):
        at = 2 * c * rows
        new_key = rotate_keys(projected[at:at + rows], cosine, sine)
        new_key = new_key.astype(jnp.bfloat16).astype(jnp.float32)
        new_value = projected[at + rows:at + 2 * rows].astype(jnp.bfloat16).astype(jnp.float32)
        for h in range(c * group_size, (c + 1) * group_size):
            fresh = jnp.sum(query32[:, h, :] * new_key, axis=1, keepdims=True) * scale
            old_peak = peak[:, h, :]
            new_peak = jnp.maximum(old_peak, fresh)
            keep = jnp.exp(old_peak - new_peak)
            fresh_raw = jnp.exp(fresh - new_peak)
            outputs.append(
                (mixed[:, h, :] * keep + fresh_raw * new_value)
                / (mass[:, h, :] * keep + fresh_raw)
            )
    out_ref[...] = jnp.concatenate(outputs, axis=1).astype(out_ref.dtype)
    for copy in ids_copies + r_copies + t_copies + low_copies + delta_copies:
        copy.wait_send()


def project(tensor_size, replica_size, hidden, queries, keys, values, lengths, ids, weight, down, up):
    rows, local = hidden.shape
    width = weight.shape[0]
    pieces = weight.shape[1] * weight.shape[2] // LANES
    blocks = local // LANES
    band = rows * pieces
    weight = (
        weight.reshape(width, 2, pieces // 2, LANES)
        .transpose(0, 2, 1, 3)
        .reshape(width * pieces, LANES)
    )
    adapters, _, rank2 = down.shape
    down = down.transpose(0, 2, 1).reshape(adapters * rank2, local)
    up = up.reshape(adapters * rank2, up.shape[3])
    t1, r1 = tensor_size - 1, replica_size - 1
    copies = 2 * t1 + 3 * r1
    vmem = pl.BlockSpec(memory_space=pltpu.VMEM)
    smem = pl.BlockSpec(memory_space=pltpu.SMEM)
    hbm = pl.BlockSpec(memory_space=pl.ANY)
    stack = (blocks * rows, LANES)
    group_rows = rows * replica_size * 32 // LANES
    return pl.pallas_call(
        functools.partial(project_kernel, tensor_size, replica_size, pieces),
        out_shape=jax.ShapeDtypeStruct(
            (rows, queries.shape[1] * queries.shape[2]), jnp.bfloat16
        ),
        in_specs=[vmem, vmem, smem, smem, hbm, hbm, hbm, hbm, hbm],
        out_specs=vmem,
        scratch_shapes=[
            pltpu.VMEM((rows, LANES), jnp.int32),
            pltpu.VMEM(keys.shape, jnp.bfloat16),
            pltpu.VMEM(values.shape, jnp.bfloat16),
            pltpu.VMEM(queries.shape, jnp.float32),
            pltpu.VMEM(queries.shape, jnp.float32),
            pltpu.VMEM(queries.shape, jnp.float32),
            pltpu.VMEM(queries.shape, jnp.float32),
            pltpu.VMEM(stack, jnp.bfloat16),
            pltpu.VMEM((t1,) + stack, jnp.bfloat16),
            pltpu.VMEM((r1,) + stack, jnp.bfloat16),
            pltpu.VMEM((r1, rows, LANES), jnp.int32),
            pltpu.VMEM((tensor_size, local * pieces, LANES), jnp.bfloat16),
            pltpu.VMEM(down.shape, jnp.bfloat16),
            pltpu.VMEM(up.shape, jnp.bfloat16),
            pltpu.VMEM((tensor_size, 2 * band, local * pieces // 2), jnp.bfloat16),
            pltpu.VMEM((2 * band, 2 * LANES), jnp.float32),
            pltpu.VMEM((group_rows, LANES), jnp.float32),
            pltpu.VMEM((t1, group_rows, LANES), jnp.float32),
            pltpu.VMEM((replica_size, band, LANES), jnp.float32),
            pltpu.VMEM((r1, band, LANES), jnp.float32),
            pltpu.SemaphoreType.DMA((6 + tensor_size,)),
            pltpu.SemaphoreType.DMA((copies,)),
            pltpu.SemaphoreType.DMA((copies,)),
        ],
        compiler_params=pltpu.CompilerParams(
            collective_id=0, has_side_effects=True, vmem_limit_bytes=58 << 20
        ),
        cost_estimate=pl.CostEstimate(
            flops=2 * rows * width * pieces * LANES,
            bytes_accessed=2 * (weight.size + down.size + up.size),
            transcendentals=0,
        ),
    )(hidden, queries, lengths, ids, keys, values, weight, down, up)


def solution(mesh):
    in_specs = (
        P(("group", "replica"), "tensor"),
        P(("group", "replica"), "tensor", None),
        P(("group", "replica"), "tensor", None, None),
        P(("group", "replica"), "tensor", None, None),
        P(("group", "replica")),
        P(("group", "replica")),
        P(None, None, "tensor"),
        P(("group", "replica"), "tensor", None),
        P(("group", "replica"), None, None, "tensor"),
    )
    out_specs = P(("group", "replica"), "tensor")
    body = functools.partial(project, mesh.shape["tensor"], mesh.shape["replica"])
    return jax.shard_map(
        body, mesh=mesh, in_specs=in_specs, out_specs=out_specs, check_vma=False
    )
```
